32 devices in a mesh: layer: 2 (over y), row: 4 (over x, core), col: 4 (over z).
Axes of the slice: x: 2, y: 2, z: 4, core: 2. Of those that a mesh axis runs over, the one named last changes fastest.
Arguments:
- inverse_rows: bfloat16 [43008, 21504], P(('layer', 'col'), 'row'), parts along dimension 0
- hess_weight: float32 [43008, 512], P(('layer', 'row', 'col')), parts along dimension 0, may hold values from -6 to 6
- pruned_start: float32 [43008, 512], P(('layer', 'row', 'col')), parts along dimension 0, may hold values from -6 to 6
- dual_start: float32 [43008, 512], P(('layer', 'row', 'col')), parts along dimension 0, may hold values from -3 to 3
- prune_mask: int32 [43008, 512], P(('layer', 'row', 'col')), parts along dimension 0, may hold values 0 or 1
- dual_rate: int32 [1024], P('layer'), parts along dimension 0, may hold values from 0 to 3
Outputs:
- repaired: float32 [43008, 512], P(('layer', 'row', 'col')), parts along dimension 0
- duals: float32 [43008, 512], P(('layer', 'row', 'col')), parts along dimension 0
The draws below stay inside these ranges and needn't reach their ends.
There are 2 independent parts, one for each index of `layer`. The reference program is written for one: setup_inputs(seed, part) draws one part's arguments, and reference() takes and returns one part's arrays. A program takes and returns all parts, laid end to end along the dimension named above; each array names one. Nothing has to cross between parts.
All inputs are finite; a program needn't handle non-finite values. No bound on the sum of `prune_mask` on one device may be relied on, other than what follows from the above.
Results may differ from the reference program's by a relative error of at most 0.0031.
Values may be sent and summed in bfloat16 or wider, within the bound.
No kernel may reach another device: no remote copies, remote signals or barrier semaphores. Data moves between devices by JAX's collectives and lax.ppermute only.
A program may use at most 256 MiB of HBM per device.

```python
import math
import jax
import jax.numpy as jnp
from jax import lax

N = 21504
OUT = 512
ITERS = 3
SHARD = 1344
SLAB = 5376
N_ROW = 4
N_COL = 4


def draw_inverse_rows(key, part):
    stored = jnp.arange(N, dtype=jnp.int32)
    group = stored // SLAB
    within = stored % SLAB
    block = within // SHARD
    offset = within % SHARD
    global_row = (block * (N // SLAB) + group) * SHARD + offset
    noise = jax.random.normal(key, (N, N), jnp.float32)
    diagonal = (global_row[:, None] == jnp.arange(N, dtype=jnp.int32)[None, :]).astype(jnp.float32)
    return (noise * (0.4 / math.sqrt(N)) + 0.5 * diagonal).astype(jnp.bfloat16)


def place_ends(result, own_key, smallest, top_value):
    spot = [jax.random.randint(jax.random.fold_in(own_key, axis), (), 0, length) for axis, length in enumerate(result.shape)]
    widest = result.shape.index(max(result.shape))
    next_to = spot[:widest] + [(spot[widest] + 1) % result.shape[widest]] + spot[widest + 1:]
    return result.at[tuple(spot)].set(smallest).at[tuple(next_to)].set(top_value)


def steps_of(rng, shape, split, smallest, largest):
    gain = 1.0
    for position, parts in split:
        steps = jax.random.uniform(jax.random.fold_in(jax.random.fold_in(rng, 6), position), (parts,), jnp.float32, smallest / len(split), largest / len(split))
        gain = gain * jnp.repeat(jnp.exp(steps), shape[position] // parts).reshape((-1,) + (1,) * (len(shape) - 1 - position))
    return gain


def normal_values(key, extent, width, most, shards=(), kind=jnp.bfloat16):
    loudness = steps_of(key, extent, shards, -0.22, 0.18) if shards else 1.0
    drawn = jax.random.normal(key, extent, jnp.float32) * width * loudness
    return jnp.minimum(jnp.maximum(drawn, -most), most).astype(kind)


def setup_inputs(seed: int = 0, part: int = 0) -> dict:
    streams_of = jax.random.split(jax.random.key(seed), 7)
    part_splits = jax.random.split(jax.random.fold_in(streams_of[6], part), 7)
    inverse_rows = draw_inverse_rows(jax.random.fold_in(jax.random.fold_in(streams_of[6], part), 71), part)
    hess_weight = normal_values(part_splits[1], (N, OUT), 1.0, 6.0, ((0, 16),), jnp.float32)
    pruned_start = normal_values(part_splits[2], (N, OUT), 1.0, 6.0, ((0, 16),), jnp.float32)
    dual_start = normal_values(part_splits[3], (N, OUT), 0.5, 3.0, ((0, 16),), jnp.float32)
    prune_mask = place_ends((jax.random.randint(part_splits[4], (N, OUT), 0, 2) < 1).astype(jnp.int32), jax.random.fold_in(part_splits[4], 1), 0, 1)
    dual_rate = place_ends(jax.random.randint(part_splits[5], (OUT,), 0, 4), jax.random.fold_in(part_splits[5], 1), 0, 3).astype(jnp.int32)
    return dict(inverse_rows=inverse_rows, hess_weight=hess_weight, pruned_start=pruned_start, dual_start=dual_start, prune_mask=prune_mask, dual_rate=dual_rate)


def reference(inverse_rows, hess_weight, pruned_start, dual_start, prune_mask, dual_rate):
    panels = inverse_rows.reshape(N_COL, N // N_COL, N)
    kept = prune_mask.astype(jnp.float32)
    step_size = 0.5 + 0.25 * dual_rate.astype(jnp.float32)
    projected = pruned_start
    scaled = dual_start
    for iteration in range(ITERS):
        right_side = (hess_weight + projected - scaled).astype(jnp.bfloat16)
        right_wide = right_side.astype(jnp.float32)

        def apply_panel(panel):
            return jnp.dot(panel.astype(jnp.float32), right_wide, preferred_element_type=jnp.float32)

        stored = lax.map(apply_panel, panels)
        iterate = stored.reshape(N_COL, N_ROW, N // (N_ROW * N_COL), OUT)
        iterate = jnp.transpose(iterate, (1, 0, 2, 3)).reshape(N, OUT)
        projected = kept * (iterate + scaled)
        scaled = scaled + step_size[None, :] * (iterate - projected)
    return projected, scaled
```

```python
import jax
import jax.numpy as jnp
from jax import lax
from jax.experimental import pallas as pl
from jax.experimental.pallas import tpu as pltpu
from jax.sharding import PartitionSpec as P

ITERS = 3
CHUNKS = 2
BF16 = jnp.bfloat16
F32 = jnp.float32

OUTER = [(0, 1), (1, 0), (2, 3), (3, 2)]
INNER = [(1, 2), (2, 1)]
SKIP = [(0, 2), (3, 1)]
ENDS = [(1, 0), (2, 3)]
CORE = [(0, 1), (1, 0), (2, 3), (3, 2)]
ACROSS = [(0, 2), (2, 0), (1, 3), (3, 1)]


def first_pair_kernel(place, matrix, own, near, out, pair, sems):
    shard = own.shape[0]

    @pl.when(pl.program_id(0) == 0)
    def _():
        here = pl.multiple_of(place[1] * shard, 16)
        there = pl.multiple_of((1 - place[1]) * shard, 16)
        copies = [
            pltpu.make_async_copy(own, pair.at[pl.ds(here, shard)], sems.at[0]),
            pltpu.make_async_copy(near, pair.at[pl.ds(there, shard)], sems.at[1]),
        ]
        for copy in copies:
            copy.start()
        for copy in copies:
            copy.wait()

    out[...] = jnp.dot(matrix[...], pair[...], preferred_element_type=F32)


def first_pair(place, matrix, own, near, tile):
    shard, width = own.shape
    slab = matrix.shape[0]
    return pl.pallas_call(
        first_pair_kernel,
        grid_spec=pltpu.PrefetchScalarGridSpec(
            num_scalar_prefetch=1,
            grid=(slab // tile,),
            in_specs=[
                pl.BlockSpec((tile, 2 * shard), lambda i, place: (i, place[0])),
                pl.BlockSpec(memory_space=pl.ANY),
                pl.BlockSpec(memory_space=pl.ANY),
            ],
            out_specs=pl.BlockSpec((tile, width), lambda i, place: (i, 0)),
            scratch_shapes=[pltpu.VMEM((2 * shard, width), BF16), pltpu.SemaphoreType.DMA((2,))],
        ),
        out_shape=jax.ShapeDtypeStruct((slab, width), F32),
        compiler_params=pltpu.CompilerParams(vmem_limit_bytes=32 * 2**20),
        cost_estimate=pl.CostEstimate(
            flops=4 * slab * shard * width, bytes_accessed=4 * slab * shard + 4 * slab * width, transcendentals=0
        ),
        name="first_pair",
    )(place, matrix, own, near)


def second_pair_kernel(place, matrix, before, end_a, end_b, mid_a, mid_b, send, keep, pair, sems):
    shard = end_a.shape[0]
    step = pl.program_id(0)
    half_steps = pl.num_programs(0) // 2

    @pl.when(step == 0)
    def _():
        here = pl.multiple_of((1 - place[0]) * shard, 16)
        there = pl.multiple_of(place[0] * shard, 16)

        def fetch(a, b):
            copies = [
                pltpu.make_async_copy(a, pair.at[pl.ds(here, shard)], sems.at[0]),
                pltpu.make_async_copy(b, pair.at[pl.ds(there, shard)], sems.at[1]),
            ]
            for copy in copies:
                copy.start()
            for copy in copies:
                copy.wait()

        @pl.when(place[1] == 1)
        def _():
            fetch(end_a, end_b)

        @pl.when(place[1] == 0)
        def _():
            fetch(mid_a, mid_b)

    total = before[...] + jnp.dot(matrix[...], pair[...], preferred_element_type=F32)

    @pl.when(step < half_steps)
    def _():
        send[...] = total.astype(BF16)

    @pl.when(step >= half_steps)
    def _():
        keep[...] = total


def second_pair(place, matrix, before, ends, mids, tile):
    shard, width = ends[0].shape
    steps = shard // tile

    def row(i, place):
        return jnp.where(i < steps, place[2], place[3]) * steps + lax.rem(i, steps)

    return pl.pallas_call(
        second_pair_kernel,
        grid_spec=pltpu.PrefetchScalarGridSpec(
            num_scalar_prefetch=1,
            grid=(2 * steps,),
            in_specs=[
                pl.BlockSpec((tile, 2 * shard), lambda i, place: (row(i, place), place[0])),
                pl.BlockSpec((tile, width), lambda i, place: (row(i, place), 0)),
            ]
            + [pl.BlockSpec(memory_space=pl.ANY)] * 4,
            out_specs=[
                pl.BlockSpec((tile, width), lambda i, place: (jnp.minimum(i, steps - 1), 0)),
                pl.BlockSpec((tile, width), lambda i, place: (jnp.maximum(i - steps, 0), 0)),
            ],
            scratch_shapes=[pltpu.VMEM((2 * shard, width), BF16), pltpu.SemaphoreType.DMA((2,))],
        ),
        out_shape=[jax.ShapeDtypeStruct((shard, width), BF16), jax.ShapeDtypeStruct((shard, width), F32)],
        compiler_params=pltpu.CompilerParams(vmem_limit_bytes=32 * 2**20),
        cost_estimate=pl.CostEstimate(
            flops=8 * shard * shard * width, bytes_accessed=8 * shard * shard + 14 * shard * width, transcendentals=0
        ),
        name="second_pair",
    )(place, matrix, before, *ends, *mids)


def pipelined(inverse_rows, hess_weight, pruned_start, dual_start, prune_mask, dual_rate):
    shard, out = hess_weight.shape
    width = out // CHUNKS
    tile = 672
    col = lax.axis_index("col")
    row = lax.axis_index("row")
    own_pair = col // 2
    at_end = (col == 0) | (col == 3)
    core = row % 2
    other_x = 1 - row // 2
    as_i32 = lambda *values: jnp.stack([jnp.asarray(value, jnp.int32) for value in values])
    first_place = as_i32(own_pair, col % 2)
    far_place = as_i32(1 - own_pair, at_end, 2 * other_x + 1 - core, 2 * other_x + core)
    near_place = as_i32(1 - own_pair, at_end, row + 1 - 2 * core, row)

    kept = prune_mask.astype(F32)
    step_size = (0.5 + 0.25 * dual_rate.astype(F32))[None, :]
    parts = [slice(chunk * width, (chunk + 1) * width) for chunk in range(CHUNKS)]
    projected = [pruned_start[:, part] for part in parts]
    scaled = [dual_start[:, part] for part in parts]
    for iteration in range(ITERS):
        for chunk, part in enumerate(parts):
            own = (hess_weight[:, part] + projected[chunk] - scaled[chunk]).astype(BF16)
            outer = lax.ppermute(own, "col", OUTER)
            inner = lax.ppermute(own, "col", INNER)
            skip = lax.ppermute(own, "col", SKIP)
            end_a = lax.ppermute(inner, "col", ENDS)
            end_b = lax.ppermute(skip, "col", ENDS)
            before = first_pair(first_place, inverse_rows, own, outer, tile)
            send, keep = second_pair(far_place, inverse_rows, before, (end_a, end_b), (inner, skip), tile)
            far = (keep + lax.ppermute(send, "row", CORE).astype(F32)).astype(BF16)
            send, keep = second_pair(near_place, inverse_rows, before, (end_a, end_b), (inner, skip), tile)
            near = keep + lax.ppermute(send, "row", CORE).astype(F32)
            iterate = near + lax.ppermute(far, "row", ACROSS).astype(F32)
            projected[chunk] = kept[:, part] * (iterate + scaled[chunk])
            scaled[chunk] = scaled[chunk] + step_size[:, part] * (iterate - projected[chunk])
    return jnp.concatenate(projected, 1), jnp.concatenate(scaled, 1)


def plain(inverse_rows, hess_weight, pruned_start, dual_start, prune_mask, dual_rate):
    kept = prune_mask.astype(F32)
    step_size = 0.5 + 0.25 * dual_rate.astype(F32)
    projected = pruned_start
    scaled = dual_start
    for iteration in range(ITERS):
        right_side = (hess_weight + projected - scaled).astype(BF16)
        partial_value = jnp.dot(
            inverse_rows,
            lax.all_gather(right_side, "col", axis=0, tiled=True),
            preferred_element_type=F32,
        )
        iterate = lax.psum_scatter(partial_value, "row", scatter_dimension=0, tiled=True)
        projected = kept * (iterate + scaled)
        scaled = scaled + step_size[None, :] * (iterate - projected)
    return (projected, scaled)


def solution(mesh):
    in_specs = (
        P(("layer", "col"), "row"),
        P(("layer", "row", "col"), None),
        P(("layer", "row", "col"), None),
        P(("layer", "row", "col"), None),
        P(("layer", "row", "col"), None),
        P("layer"),
    )
    out_specs = (P(("layer", "row", "col"), None), P(("layer", "row", "col"), None))
    four_by_four = mesh.shape["row"] == 4 and mesh.shape["col"] == 4
    local = pipelined if four_by_four else plain
    return jax.shard_map(local, mesh=mesh, in_specs=in_specs, out_specs=out_specs, check_vma=False)
```

```python
import jax
import jax.numpy as jnp
from jax import lax
from jax.experimental import pallas as pl
from jax.experimental.pallas import tpu as pltpu
from jax.sharding import PartitionSpec as P

ITERS = 3
CHUNKS = 2
BF16 = jnp.bfloat16
F32 = jnp.float32

OUTER = [(0, 1), (1, 0), (2, 3), (3, 2)]
INNER = [(1, 2), (2, 1)]
SKIP = [(0, 2), (3, 1)]
ENDS = [(1, 0), (2, 3)]
CORE = [(0, 1), (1, 0), (2, 3), (3, 2)]
ACROSS = [(0, 2), (2, 0), (1, 3), (3, 1)]


def first_pair_kernel(place, matrix, own, near, after, out, pair, sems):
    shard = own.shape[0]

    @pl.when(pl.program_id(0) == 0)
    def _():
        here = pl.multiple_of(place[1] * shard, 16)
        there = pl.multiple_of((1 - place[1]) * shard, 16)
        copies = [
            pltpu.make_async_copy(own, pair.at[pl.ds(here, shard)], sems.at[0]),
            pltpu.make_async_copy(near, pair.at[pl.ds(there, shard)], sems.at[1]),
        ]
        for copy in copies:
            copy.start()
        for copy in copies:
            copy.wait()

    out[...] = jnp.dot(matrix[...], pair[...], preferred_element_type=F32)


def first_pair(place, matrix, own, near, after, tile):
    shard, width = own.shape
    slab = matrix.shape[0]
    return pl.pallas_call(
        first_pair_kernel,
        grid_spec=pltpu.PrefetchScalarGridSpec(
            num_scalar_prefetch=1,
            grid=(slab // tile,),
            in_specs=[
                pl.BlockSpec((tile, 2 * shard), lambda i, place: (i, place[0])),
                pl.BlockSpec(memory_space=pl.ANY),
                pl.BlockSpec(memory_space=pl.ANY),
                pl.BlockSpec(memory_space=pl.ANY),
            ],
            out_specs=pl.BlockSpec((tile, width), lambda i, place: (i, 0)),
            scratch_shapes=[pltpu.VMEM((2 * shard, width), BF16), pltpu.SemaphoreType.DMA((2,))],
        ),
        out_shape=jax.ShapeDtypeStruct((slab, width), F32),
        compiler_params=pltpu.CompilerParams(vmem_limit_bytes=32 * 2**20),
        cost_estimate=pl.CostEstimate(
            flops=4 * slab * shard * width, bytes_accessed=4 * slab * shard + 4 * slab * width, transcendentals=0
        ),
        name="first_pair",
    )(place, matrix, own, near, after)


def second_pair_kernel(place, matrix, before, end_a, end_b, mid_a, mid_b, after, send, keep, pair, sems):
    shard = end_a.shape[0]
    step = pl.program_id(0)
    half_steps = pl.num_programs(0) // 2

    @pl.when(step == 0)
    def _():
        here = pl.multiple_of((1 - place[0]) * shard, 16)
        there = pl.multiple_of(place[0] * shard, 16)

        def fetch(a, b):
            copies = [
                pltpu.make_async_copy(a, pair.at[pl.ds(here, shard)], sems.at[0]),
                pltpu.make_async_copy(b, pair.at[pl.ds(there, shard)], sems.at[1]),
            ]
            for copy in copies:
                copy.start()
            for copy in copies:
                copy.wait()

        @pl.when(place[1] == 1)
        def _():
            fetch(end_a, end_b)

        @pl.when(place[1] == 0)
        def _():
            fetch(mid_a, mid_b)

    total = before[...] + jnp.dot(matrix[...], pair[...], preferred_element_type=F32)

    @pl.when(step < half_steps)
    def _():
        send[...] = total.astype(BF16)

    @pl.when(step >= half_steps)
    def _():
        keep[...] = total


def second_pair(place, matrix, before, ends, mids, after, tile):
    shard, width = ends[0].shape
    steps = shard // tile

    def row(i, place):
        return jnp.where(i < steps, place[2], place[3]) * steps + lax.rem(i, steps)

    return pl.pallas_call(
        second_pair_kernel,
        grid_spec=pltpu.PrefetchScalarGridSpec(
            num_scalar_prefetch=1,
            grid=(2 * steps,),
            in_specs=[
                pl.BlockSpec((tile, 2 * shard), lambda i, place: (row(i, place), place[0])),
                pl.BlockSpec((tile, width), lambda i, place: (row(i, place), 0)),
            ]
            + [pl.BlockSpec(memory_space=pl.ANY)] * 5,
            out_specs=[
                pl.BlockSpec((tile, width), lambda i, place: (jnp.minimum(i, steps - 1), 0)),
                pl.BlockSpec((tile, width), lambda i, place: (jnp.maximum(i - steps, 0), 0)),
            ],
            scratch_shapes=[pltpu.VMEM((2 * shard, width), BF16), pltpu.SemaphoreType.DMA((2,))],
        ),
        out_shape=[jax.ShapeDtypeStruct((shard, width), BF16), jax.ShapeDtypeStruct((shard, width), F32)],
        compiler_params=pltpu.CompilerParams(vmem_limit_bytes=32 * 2**20),
        cost_estimate=pl.CostEstimate(
            flops=8 * shard * shard * width, bytes_accessed=8 * shard * shard + 14 * shard * width, transcendentals=0
        ),
        name="second_pair",
    )(place, matrix, before, *ends, *mids, after)


def pipelined(inverse_rows, hess_weight, pruned_start, dual_start, prune_mask, dual_rate):
    shard, out = hess_weight.shape
    width = out // CHUNKS
    tile = 672
    col = lax.axis_index("col")
    row = lax.axis_index("row")
    own_pair = col // 2
    at_end = (col == 0) | (col == 3)
    core = row % 2
    other_x = 1 - row // 2
    as_i32 = lambda *values: jnp.stack([jnp.asarray(value, jnp.int32) for value in values])
    first_place = as_i32(own_pair, col % 2)
    far_place = as_i32(1 - own_pair, at_end, 2 * other_x + 1 - core, 2 * other_x + core)
    near_place = as_i32(1 - own_pair, at_end, row + 1 - 2 * core, row)

    kept = prune_mask.astype(F32)
    step_size = (0.5 + 0.25 * dual_rate.astype(F32))[None, :]
    parts = [slice(chunk * width, (chunk + 1) * width) for chunk in range(CHUNKS)]
    projected = [pruned_start[:, part] for part in parts]
    scaled = [dual_start[:, part] for part in parts]

    def right_side(chunk):
        return (hess_weight[:, parts[chunk]] + projected[chunk] - scaled[chunk]).astype(BF16)

    def gather(own):
        outer = lax.ppermute(own, "col", OUTER)
        inner = lax.ppermute(own, "col", INNER)
        skip = lax.ppermute(own, "col", SKIP)
        end_a = lax.ppermute(inner, "col", ENDS)
        end_b = lax.ppermute(skip, "col", ENDS)
        return own, outer, (end_a, end_b), (inner, skip)

    def multiply_first(gathered, after):
        own, outer, _, _ = gathered
        return first_pair(first_place, inverse_rows, own, outer, after, 1344)

    def multiply_rest(gathered, before, after):
        _, _, ends, mids = gathered
        send_far, keep_far = second_pair(far_place, inverse_rows, before, ends, mids, after, tile)
        send_near, keep_near = second_pair(near_place, inverse_rows, before, ends, mids, keep_far, tile)
        far = (keep_far + lax.ppermute(send_far, "row", CORE).astype(F32)).astype(BF16)
        return far, keep_near, lax.ppermute(send_near, "row", CORE), lax.ppermute(far, "row", ACROSS)

    def update(chunk, reduced):
        _, near, core_sum, far_sum = reduced
        iterate = near + core_sum.astype(F32) + far_sum.astype(F32)
        projected[chunk] = kept[:, parts[chunk]] * (iterate + scaled[chunk])
        scaled[chunk] = scaled[chunk] + step_size[:, parts[chunk]] * (iterate - projected[chunk])

    gathered = gather(right_side(0))
    before = multiply_first(gathered, gathered[0])
    after = before
    waiting = right_side(1)
    waiting, _ = lax.optimization_barrier((waiting, gathered[3][1]))
    for step in range(ITERS * CHUNKS):
        chunk, last = step % CHUNKS, step == ITERS * CHUNKS - 1
        upcoming = None if last else gather(waiting)
        reduced = multiply_rest(gathered, before, after)
        if not last:
            before = multiply_first(upcoming, reduced[0])
        update(chunk, reduced)
        waiting = after = right_side(chunk)
        gathered = upcoming
    return jnp.concatenate(projected, 1), jnp.concatenate(scaled, 1)


def plain(inverse_rows, hess_weight, pruned_start, dual_start, prune_mask, dual_rate):
    kept = prune_mask.astype(F32)
    step_size = 0.5 + 0.25 * dual_rate.astype(F32)
    projected = pruned_start
    scaled = dual_start
    for iteration in range(ITERS):
        right_side = (hess_weight + projected - scaled).astype(BF16)
        partial_value = jnp.dot(
            inverse_rows,
            lax.all_gather(right_side, "col", axis=0, tiled=True),
            preferred_element_type=F32,
        )
        iterate = lax.psum_scatter(partial_value, "row", scatter_dimension=0, tiled=True)
        projected = kept * (iterate + scaled)
        scaled = scaled + step_size[None, :] * (iterate - projected)
    return (projected, scaled)


def solution(mesh):
    in_specs = (
        P(("layer", "col"), "row"),
        P(("layer", "row", "col"), None),
        P(("layer", "row", "col"), None),
        P(("layer", "row", "col"), None),
        P(("layer", "row", "col"), None),
        P("layer"),
    )
    out_specs = (P(("layer", "row", "col"), None), P(("layer", "row", "col"), None))
    four_by_four = mesh.shape["row"] == 4 and mesh.shape["col"] == 4
    local = pipelined if four_by_four else plain
    return jax.shard_map(local, mesh=mesh, in_specs=in_specs, out_specs=out_specs, check_vma=False)
```

```python
import jax
import jax.numpy as jnp
from jax import lax
from jax.experimental import pallas as pl
from jax.experimental.pallas import tpu as pltpu
from jax.sharding import PartitionSpec as P

ITERS = 3
CHUNKS = 2
BF16 = jnp.bfloat16
F32 = jnp.float32

OUTER = [(0, 1), (1, 0), (2, 3), (3, 2)]
INNER = [(1, 2), (2, 1)]
ENDS = [(1, 0), (2, 3)]
CORE = [(0, 1), (1, 0), (2, 3), (3, 2)]
ACROSS = [(0, 2), (2, 0), (1, 3), (3, 1)]


def first_pair_kernel(place, matrix, own, near, *rest):
    out, token, pair, sems = rest[-4:]

    shard = own.shape[0]

    @pl.when(pl.program_id(0) == 0)
    def _():
        here = pl.multiple_of(place[1] * shard, 16)
        there = pl.multiple_of((1 - place[1]) * shard, 16)
        copies = [
            pltpu.make_async_copy(own, pair.at[pl.ds(here, shard)], sems.at[0]),
            pltpu.make_async_copy(near, pair.at[pl.ds(there, shard)], sems.at[1]),
        ]
        for copy in copies:
            copy.start()
        for copy in copies:
            copy.wait()

    out[...] = jnp.dot(matrix[...], pair[...], preferred_element_type=F32)
    token[...] = jnp.zeros_like(token)


def first_pair(place, matrix, own, near, after, tile):
    shard, width = own.shape
    slab = matrix.shape[0]
    return pl.pallas_call(
        first_pair_kernel,
        grid_spec=pltpu.PrefetchScalarGridSpec(
            num_scalar_prefetch=1,
            grid=(slab // tile,),
            in_specs=[
                pl.BlockSpec((tile, 2 * shard), lambda i, place: (i, place[0])),
            ]
            + [pl.BlockSpec(memory_space=pl.ANY)] * (2 + len(after)),
            out_specs=[
                pl.BlockSpec((tile, width), lambda i, place: (i, 0)),
                pl.BlockSpec((1, width), lambda i, place: (0, 0)),
            ],
            scratch_shapes=[pltpu.VMEM((2 * shard, width), BF16), pltpu.SemaphoreType.DMA((2,))],
        ),
        out_shape=[jax.ShapeDtypeStruct((slab, width), F32), jax.ShapeDtypeStruct((1, width), F32)],
        compiler_params=pltpu.CompilerParams(vmem_limit_bytes=20 * 2**20),
        cost_estimate=pl.CostEstimate(
            flops=4 * slab * shard * width, bytes_accessed=4 * slab * shard + 4 * slab * width, transcendentals=0
        ),
        name="first_pair",
    )(place, matrix, own, near, *after)


def second_pair_kernel(place, matrix, before, end_a, end_b, mid_a, mid_b, after, send, keep, pair, sems):
    shard = end_a.shape[0]
    step = pl.program_id(0)
    half_steps = pl.num_programs(0) // 2

    @pl.when(step == 0)
    def _():
        here = pl.multiple_of((1 - place[0]) * shard, 16)
        there = pl.multiple_of(place[0] * shard, 16)

        def fetch(a, b):
            copies = [
                pltpu.make_async_copy(a, pair.at[pl.ds(here, shard)], sems.at[0]),
                pltpu.make_async_copy(b, pair.at[pl.ds(there, shard)], sems.at[1]),
            ]
            for copy in copies:
                copy.start()
            for copy in copies:
                copy.wait()

        @pl.when(place[1] == 1)
        def _():
            fetch(end_a, end_b)

        @pl.when(place[1] == 0)
        def _():
            fetch(mid_a, mid_b)

    total = before[...] + jnp.dot(matrix[...], pair[...], preferred_element_type=F32)

    @pl.when(step < half_steps)
    def _():
        send[...] = total.astype(BF16)

    @pl.when(step >= half_steps)
    def _():
        keep[...] = total


def second_pair(place, matrix, before, ends, mids, after, tile):
    shard, width = ends[0].shape
    steps = shard // tile

    def row(i, place):
        return jnp.where(i < steps, place[2], place[3]) * steps + lax.rem(i, steps)

    return pl.pallas_call(
        second_pair_kernel,
        grid_spec=pltpu.PrefetchScalarGridSpec(
            num_scalar_prefetch=1,
            grid=(2 * steps,),
            in_specs=[
                pl.BlockSpec((tile, 2 * shard), lambda i, place: (row(i, place), place[0])),
                pl.BlockSpec((tile, width), lambda i, place: (row(i, place), 0)),
            ]
            + [pl.BlockSpec(memory_space=pl.ANY)] * 5,
            out_specs=[
                pl.BlockSpec((tile, width), lambda i, place: (jnp.minimum(i, steps - 1), 0)),
                pl.BlockSpec((tile, width), lambda i, place: (jnp.maximum(i - steps, 0), 0)),
            ],
            scratch_shapes=[pltpu.VMEM((2 * shard, width), BF16), pltpu.SemaphoreType.DMA((2,))],
        ),
        out_shape=[jax.ShapeDtypeStruct((shard, width), BF16), jax.ShapeDtypeStruct((shard, width), F32)],
        compiler_params=pltpu.CompilerParams(vmem_limit_bytes=14 * 2**20),
        cost_estimate=pl.CostEstimate(
            flops=8 * shard * shard * width, bytes_accessed=8 * shard * shard + 14 * shard * width, transcendentals=0
        ),
        name="second_pair",
    )(place, matrix, before, *ends, *mids, after)


def hold_kernel(*refs):
    refs[-1][...] = jnp.zeros_like(refs[-1])


def hold(width, *others):
    return pl.pallas_call(
        hold_kernel,
        in_specs=[pl.BlockSpec(memory_space=pl.ANY)] * len(others),
        out_specs=pl.BlockSpec(memory_space=pltpu.VMEM),
        out_shape=jax.ShapeDtypeStruct((1, width), F32),
        compiler_params=pltpu.CompilerParams(vmem_limit_bytes=2**20),
        name="hold",
    )(*others)


def pipelined(inverse_rows, hess_weight, pruned_start, dual_start, prune_mask, dual_rate):
    shard, out = hess_weight.shape
    width = out // CHUNKS
    tile = 672
    col = lax.axis_index("col")
    row = lax.axis_index("row")
    own_pair = col // 2
    at_end = (col == 0) | (col == 3)
    core = row % 2
    other_x = 1 - row // 2
    as_i32 = lambda *values: jnp.stack([jnp.asarray(value, jnp.int32) for value in values])
    first_place = as_i32(own_pair, col % 2)
    far_place = as_i32(1 - own_pair, at_end, 2 * other_x + 1 - core, 2 * other_x + core)
    near_place = as_i32(1 - own_pair, at_end, row + 1 - 2 * core, row)

    kept = prune_mask.astype(F32)
    step_size = (0.5 + 0.25 * dual_rate.astype(F32))[None, :]
    parts = [slice(chunk * width, (chunk + 1) * width) for chunk in range(CHUNKS)]
    projected = [pruned_start[:, part] for part in parts]
    scaled = [dual_start[:, part] for part in parts]

    def right_side(chunk):
        return (hess_weight[:, parts[chunk]] + projected[chunk] - scaled[chunk]).astype(BF16)

    def gather(own):
        outer = lax.ppermute(own, "col", OUTER)
        inner = lax.ppermute(own, "col", INNER)
        next_inner = lax.ppermute(outer, "col", INNER)
        end_a = lax.ppermute(inner, "col", ENDS)
        end_b = lax.ppermute(next_inner, "col", ENDS)
        return own, outer, (end_a, end_b), (inner, next_inner)

    def multiply_first(gathered, after):
        own, outer, _, _ = gathered
        return first_pair(first_place, inverse_rows, own, outer, after, 1344)

    def multiply_rest(gathered, before, after, upcoming):
        _, _, ends, mids = gathered
        send_far, keep_far = second_pair(far_place, inverse_rows, before, ends, mids, after, tile)
        far = keep_far + lax.ppermute(send_far, "row", CORE).astype(F32)
        if upcoming is not None:
            far = far + hold(width, upcoming[1], upcoming[3][0])
        far = far.astype(BF16)
        send_near, keep_near = second_pair(near_place, inverse_rows, before, ends, mids, far, tile)
        return send_near, keep_near, lax.ppermute(send_near, "row", CORE), lax.ppermute(far, "row", ACROSS)

    def update(chunk, reduced, ahead):
        _, near, core_sum, far_sum = reduced
        step = step_size[:, parts[chunk]]
        for zeros in ahead:
            step = step + zeros
        iterate = near + core_sum.astype(F32) + far_sum.astype(F32)
        projected[chunk] = kept[:, parts[chunk]] * (iterate + scaled[chunk])
        scaled[chunk] = scaled[chunk] + step * (iterate - projected[chunk])

    gathered = gather(right_side(0))
    before, after = multiply_first(gathered, (gathered[3][0],))
    waiting = (right_side(1).astype(F32) + after).astype(BF16)
    for step in range(ITERS * CHUNKS):
        chunk, last = step % CHUNKS, step == ITERS * CHUNKS - 1
        upcoming = None if last else gather(waiting)
        reduced = multiply_rest(gathered, before, after, upcoming)
        if not last:
            _, _, _, far_sum = reduced
            before, token = multiply_first(upcoming, (reduced[0], far_sum, upcoming[2][0], upcoming[3][1]))
        update(chunk, reduced, () if last else (token,))
        waiting = after = right_side(chunk)
        gathered = upcoming
    return jnp.concatenate(projected, 1), jnp.concatenate(scaled, 1)


def plain(inverse_rows, hess_weight, pruned_start, dual_start, prune_mask, dual_rate):
    kept = prune_mask.astype(F32)
    step_size = 0.5 + 0.25 * dual_rate.astype(F32)
    projected = pruned_start
    scaled = dual_start
    for iteration in range(ITERS):
        right_side = (hess_weight + projected - scaled).astype(BF16)
        partial_value = jnp.dot(
            inverse_rows,
            lax.all_gather(right_side, "col", axis=0, tiled=True),
            preferred_element_type=F32,
        )
        iterate = lax.psum_scatter(partial_value, "row", scatter_dimension=0, tiled=True)
        projected = kept * (iterate + scaled)
        scaled = scaled + step_size[None, :] * (iterate - projected)
    return (projected, scaled)


def solution(mesh):
    in_specs = (
        P(("layer", "col"), "row"),
        P(("layer", "row", "col"), None),
        P(("layer", "row", "col"), None),
        P(("layer", "row", "col"), None),
        P(("layer", "row", "col"), None),
        P("layer"),
    )
    out_specs = (P(("layer", "row", "col"), None), P(("layer", "row", "col"), None))
    four_by_four = mesh.shape["row"] == 4 and mesh.shape["col"] == 4
    local = pipelined if four_by_four else plain
    return jax.shard_map(local, mesh=mesh, in_specs=in_specs, out_specs=out_specs, check_vma=False)
```

```python
import jax
import jax.numpy as jnp
from jax import lax
from jax.experimental import pallas as pl
from jax.experimental.pallas import tpu as pltpu
from jax.sharding import PartitionSpec as P

ITERS = 3
CHUNKS = 2
BF16 = jnp.bfloat16
F32 = jnp.float32

OUTER = [(0, 1), (1, 0), (2, 3), (3, 2)]
INNER = [(1, 2), (2, 1)]
ENDS = [(1, 0), (2, 3)]
CORE = [(0, 1), (1, 0), (2, 3), (3, 2)]
ACROSS = [(0, 2), (2, 0), (1, 3), (3, 1)]


def first_pair_kernel(place, matrix, own, near, *rest):
    out, token, pair, sems = rest[-4:]

    shard = own.shape[0]

    @pl.when(pl.program_id(0) == 0)
    def _():
        here = pl.multiple_of(place[1] * shard, 16)
        there = pl.multiple_of((1 - place[1]) * shard, 16)
        copies = [
            pltpu.make_async_copy(own, pair.at[pl.ds(here, shard)], sems.at[0]),
            pltpu.make_async_copy(near, pair.at[pl.ds(there, shard)], sems.at[1]),
        ]
        for copy in copies:
            copy.start()
        for copy in copies:
            copy.wait()

    out[...] = jnp.dot(matrix[...], pair[...], preferred_element_type=F32)
    token[...] = jnp.zeros_like(token)


def first_pair(place, matrix, own, near, after, tile):
    shard, width = own.shape
    slab = matrix.shape[0]
    return pl.pallas_call(
        first_pair_kernel,
        grid_spec=pltpu.PrefetchScalarGridSpec(
            num_scalar_prefetch=1,
            grid=(slab // tile,),
            in_specs=[
                pl.BlockSpec((tile, 2 * shard), lambda i, place: (i, place[0])),
            ]
            + [pl.BlockSpec(memory_space=pl.ANY)] * (2 + len(after)),
            out_specs=[
                pl.BlockSpec((tile, width), lambda i, place: (i, 0)),
                pl.BlockSpec((1, width), lambda i, place: (0, 0)),
            ],
            scratch_shapes=[pltpu.VMEM((2 * shard, width), BF16), pltpu.SemaphoreType.DMA((2,))],
        ),
        out_shape=[jax.ShapeDtypeStruct((slab, width), F32), jax.ShapeDtypeStruct((1, width), F32)],
        compiler_params=pltpu.CompilerParams(vmem_limit_bytes=20 * 2**20),
        cost_estimate=pl.CostEstimate(
            flops=4 * slab * shard * width, bytes_accessed=4 * slab * shard + 4 * slab * width, transcendentals=0
        ),
        name="first_pair",
    )(place, matrix, own, near, *after)


def second_pair_kernel(place, matrix, before, end_a, end_b, mid_a, mid_b, after, send, keep, token, pair, sems):
    shard = end_a.shape[0]
    step = pl.program_id(0)
    half_steps = pl.num_programs(0) // 2

    @pl.when(step == 0)
    def _():
        here = pl.multiple_of((1 - place[0]) * shard, 16)
        there = pl.multiple_of(place[0] * shard, 16)

        def fetch(a, b):
            copies = [
                pltpu.make_async_copy(a, pair.at[pl.ds(here, shard)], sems.at[0]),
                pltpu.make_async_copy(b, pair.at[pl.ds(there, shard)], sems.at[1]),
            ]
            for copy in copies:
                copy.start()
            for copy in copies:
                copy.wait()

        @pl.when(place[1] == 1)
        def _():
            fetch(end_a, end_b)

        @pl.when(place[1] == 0)
        def _():
            fetch(mid_a, mid_b)

    token[...] = jnp.zeros_like(token)
    total = before[...] + jnp.dot(matrix[...], pair[...], preferred_element_type=F32)

    @pl.when(step < half_steps)
    def _():
        send[...] = total.astype(BF16)

    @pl.when(step >= half_steps)
    def _():
        keep[...] = total


def second_pair(place, matrix, before, ends, mids, after, tile):
    shard, width = ends[0].shape
    steps = shard // tile

    def row(i, place):
        return jnp.where(i < steps, place[2], place[3]) * steps + lax.rem(i, steps)

    return pl.pallas_call(
        second_pair_kernel,
        grid_spec=pltpu.PrefetchScalarGridSpec(
            num_scalar_prefetch=1,
            grid=(2 * steps,),
            in_specs=[
                pl.BlockSpec((tile, 2 * shard), lambda i, place: (row(i, place), place[0])),
                pl.BlockSpec((tile, width), lambda i, place: (row(i, place), 0)),
            ]
            + [pl.BlockSpec(memory_space=pl.ANY)] * 5,
            out_specs=[
                pl.BlockSpec((tile, width), lambda i, place: (jnp.minimum(i, steps - 1), 0)),
                pl.BlockSpec((tile, width), lambda i, place: (jnp.maximum(i - steps, 0), 0)),
                pl.BlockSpec((1, width), lambda i, place: (0, 0)),
            ],
            scratch_shapes=[pltpu.VMEM((2 * shard, width), BF16), pltpu.SemaphoreType.DMA((2,))],
        ),
        out_shape=[
            jax.ShapeDtypeStruct((shard, width), BF16),
            jax.ShapeDtypeStruct((shard, width), F32),
            jax.ShapeDtypeStruct((1, width), F32),
        ],
        compiler_params=pltpu.CompilerParams(vmem_limit_bytes=14 * 2**20),
        cost_estimate=pl.CostEstimate(
            flops=8 * shard * shard * width, bytes_accessed=8 * shard * shard + 14 * shard * width, transcendentals=0
        ),
        name="second_pair",
    )(place, matrix, before, *ends, *mids, after)


def hold_kernel(*refs):
    refs[-1][...] = jnp.zeros_like(refs[-1])


def hold(width, *others):
    return pl.pallas_call(
        hold_kernel,
        in_specs=[pl.BlockSpec(memory_space=pl.ANY)] * len(others),
        out_specs=pl.BlockSpec(memory_space=pltpu.VMEM),
        out_shape=jax.ShapeDtypeStruct((1, width), F32),
        compiler_params=pltpu.CompilerParams(vmem_limit_bytes=2**20),
        name="hold",
    )(*others)


def pipelined(inverse_rows, hess_weight, pruned_start, dual_start, prune_mask, dual_rate):
    shard, out = hess_weight.shape
    width = out // CHUNKS
    tile = 672
    col = lax.axis_index("col")
    row = lax.axis_index("row")
    own_pair = col // 2
    at_end = (col == 0) | (col == 3)
    core = row % 2
    other_x = 1 - row // 2
    as_i32 = lambda *values: jnp.stack([jnp.asarray(value, jnp.int32) for value in values])
    first_place = as_i32(own_pair, col % 2)
    far_place = as_i32(1 - own_pair, at_end, 2 * other_x + 1 - core, 2 * other_x + core)
    near_place = as_i32(1 - own_pair, at_end, row + 1 - 2 * core, row)

    step_size = (0.5 + 0.25 * dual_rate.astype(F32))[None, :]
    parts = [slice(chunk * width, (chunk + 1) * width) for chunk in range(CHUNKS)]
    projected = [pruned_start[:, part] for part in parts]
    scaled = [dual_start[:, part] for part in parts]

    def right_side(chunk):
        return (hess_weight[:, parts[chunk]] + projected[chunk] - scaled[chunk]).astype(BF16)

    def gather(own):
        outer = lax.ppermute(own, "col", OUTER)
        inner = lax.ppermute(own, "col", INNER)
        next_inner = lax.ppermute(outer, "col", INNER)
        end_a = lax.ppermute(inner, "col", ENDS)
        return own, outer, end_a, (inner, next_inner)

    def finish(gathered, zeros):
        own, outer, end_a, (inner, next_inner) = gathered
        passed = (next_inner.astype(F32) + zeros).astype(BF16)
        end_b = lax.ppermute(passed, "col", ENDS)
        return own, outer, (end_a, end_b), (inner, next_inner)

    def multiply_rest(gathered, before, after, upcoming):
        _, _, ends, mids = gathered
        send_far, keep_far, _ = second_pair(far_place, inverse_rows, before, ends, mids, after, tile)
        far = keep_far + lax.ppermute(send_far, "row", CORE).astype(F32)
        if upcoming is not None:
            far = far + hold(width, upcoming[1], upcoming[3][0])
        far = far.astype(BF16)
        send_near, keep_near, zeros = second_pair(near_place, inverse_rows, before, ends, mids, far, tile)
        sums = keep_near, lax.ppermute(send_near, "row", CORE), lax.ppermute(far, "row", ACROSS)
        return sums, send_near, zeros

    def update(chunk, sums, zeros):
        near, core_sum, far_sum = sums
        step = step_size[:, parts[chunk]] + zeros
        iterate = near + core_sum.astype(F32) + far_sum.astype(F32)
        projected[chunk] = jnp.where(prune_mask[:, parts[chunk]] == 1, iterate + scaled[chunk], 0.0)
        scaled[chunk] = scaled[chunk] + step * (iterate - projected[chunk])

    gathered = gather(right_side(0))
    before, after = first_pair(first_place, inverse_rows, *gathered[:2], (gathered[3][0],), 1344)
    gathered = finish(gathered, 0.0)
    waiting = (right_side(1).astype(F32) + after).astype(BF16)
    for step in range(ITERS * CHUNKS):
        chunk, last = step % CHUNKS, step == ITERS * CHUNKS - 1
        upcoming = None if last else gather(waiting)
        sums, sent, zeros = multiply_rest(gathered, before, after, upcoming)
        if last:
            zeros = hold(width, sums[2])
        else:
            unread = (sent, sums[2], upcoming[2], upcoming[3][1])
            before, after_first = first_pair(first_place, inverse_rows, *upcoming[:2], unread, 1344)
            gathered = finish(upcoming, zeros)
            zeros = after_first
        update(chunk, sums, zeros)
        waiting = after = right_side(chunk)
    whole = [jnp.pad(half[0], ((0, 0), (0, width))) for half in (projected, scaled)]
    return tuple(
        lax.dynamic_update_slice(full, half[1], (0, width)) for full, half in zip(whole, (projected, scaled))
    )


def plain(inverse_rows, hess_weight, pruned_start, dual_start, prune_mask, dual_rate):
    kept = prune_mask.astype(F32)
    step_size = 0.5 + 0.25 * dual_rate.astype(F32)
    projected = pruned_start
    scaled = dual_start
    for iteration in range(ITERS):
        right_side = (hess_weight + projected - scaled).astype(BF16)
        partial_value = jnp.dot(
            inverse_rows,
            lax.all_gather(right_side, "col", axis=0, tiled=True),
            preferred_element_type=F32,
        )
        iterate = lax.psum_scatter(partial_value, "row", scatter_dimension=0, tiled=True)
        projected = kept * (iterate + scaled)
        scaled = scaled + step_size[None, :] * (iterate - projected)
    return (projected, scaled)


def solution(mesh):
    in_specs = (
        P(("layer", "col"), "row"),
        P(("layer", "row", "col"), None),
        P(("layer", "row", "col"), None),
        P(("layer", "row", "col"), None),
        P(("layer", "row", "col"), None),
        P("layer"),
    )
    out_specs = (P(("layer", "row", "col"), None), P(("layer", "row", "col"), None))
    four_by_four = mesh.shape["row"] == 4 and mesh.shape["col"] == 4
    local = pipelined if four_by_four else plain
    return jax.shard_map(local, mesh=mesh, in_specs=in_specs, out_specs=out_specs, check_vma=False)
```

```python
import jax
import jax.numpy as jnp
from jax import lax
from jax.experimental import pallas as pl
from jax.experimental.pallas import tpu as pltpu
from jax.sharding import PartitionSpec as P

ITERS = 3
CHUNKS = 2
BF16 = jnp.bfloat16
F32 = jnp.float32

OUTER = [(0, 1), (1, 0), (2, 3), (3, 2)]
INNER = [(1, 2), (2, 1)]
ENDS = [(1, 0), (2, 3)]
CORE = [(0, 1), (1, 0), (2, 3), (3, 2)]
ACROSS = [(0, 2), (2, 0), (1, 3), (3, 1)]


def first_pair_kernel(place, matrix, own, near, *rest):
    out, token, pair, sems = rest[-4:]

    shard = own.shape[0]

    @pl.when(pl.program_id(0) == 0)
    def _():
        here = pl.multiple_of(place[1] * shard, 16)
        there = pl.multiple_of((1 - place[1]) * shard, 16)
        copies = [
            pltpu.make_async_copy(own, pair.at[pl.ds(here, shard)], sems.at[0]),
            pltpu.make_async_copy(near, pair.at[pl.ds(there, shard)], sems.at[1]),
        ]
        for copy in copies:
            copy.start()
        for copy in copies:
            copy.wait()

    out[...] = jnp.dot(matrix[...], pair[...], preferred_element_type=F32)
    token[...] = jnp.zeros_like(token)


def first_pair(place, matrix, own, near, after, tile):
    shard, width = own.shape
    slab = matrix.shape[0]
    return pl.pallas_call(
        first_pair_kernel,
        grid_spec=pltpu.PrefetchScalarGridSpec(
            num_scalar_prefetch=1,
            grid=(slab // tile,),
            in_specs=[
                pl.BlockSpec((tile, 2 * shard), lambda i, place: (i, place[0])),
            ]
            + [pl.BlockSpec(memory_space=pl.ANY)] * (2 + len(after)),
            out_specs=[
                pl.BlockSpec((tile, width), lambda i, place: (i, 0)),
                pl.BlockSpec((1, width), lambda i, place: (0, 0)),
            ],
            scratch_shapes=[pltpu.VMEM((2 * shard, width), BF16), pltpu.SemaphoreType.DMA((2,))],
        ),
        out_shape=[jax.ShapeDtypeStruct((slab, width), F32), jax.ShapeDtypeStruct((1, width), F32)],
        compiler_params=pltpu.CompilerParams(vmem_limit_bytes=20 * 2**20),
        cost_estimate=pl.CostEstimate(
            flops=4 * slab * shard * width, bytes_accessed=4 * slab * shard + 4 * slab * width, transcendentals=0
        ),
        name="first_pair",
    )(place, matrix, own, near, *after)


def second_pair_kernel(place, matrix, before, end_a, end_b, mid_a, mid_b, after, send, keep, token, pair, sems):
    shard = end_a.shape[0]
    step = pl.program_id(0)
    half_steps = pl.num_programs(0) // 2

    @pl.when(step == 0)
    def _():
        here = pl.multiple_of((1 - place[0]) * shard, 16)
        there = pl.multiple_of(place[0] * shard, 16)

        def fetch(a, b):
            copies = [
                pltpu.make_async_copy(a, pair.at[pl.ds(here, shard)], sems.at[0]),
                pltpu.make_async_copy(b, pair.at[pl.ds(there, shard)], sems.at[1]),
            ]
            for copy in copies:
                copy.start()
            for copy in copies:
                copy.wait()

        @pl.when(place[1] == 1)
        def _():
            fetch(end_a, end_b)

        @pl.when(place[1] == 0)
        def _():
            fetch(mid_a, mid_b)

    token[...] = jnp.zeros_like(token)
    total = before[...] + jnp.dot(matrix[...], pair[...], preferred_element_type=F32)

    @pl.when(step < half_steps)
    def _():
        send[...] = total.astype(BF16)

    @pl.when(step >= half_steps)
    def _():
        keep[...] = total


def second_pair(place, matrix, before, ends, mids, after, tile):
    shard, width = ends[0].shape
    steps = shard // tile

    def row(i, place):
        return jnp.where(i < steps, place[2], place[3]) * steps + lax.rem(i, steps)

    return pl.pallas_call(
        second_pair_kernel,
        grid_spec=pltpu.PrefetchScalarGridSpec(
            num_scalar_prefetch=1,
            grid=(2 * steps,),
            in_specs=[
                pl.BlockSpec((tile, 2 * shard), lambda i, place: (row(i, place), place[0])),
                pl.BlockSpec((tile, width), lambda i, place: (row(i, place), 0)),
            ]
            + [pl.BlockSpec(memory_space=pl.ANY)] * 5,
            out_specs=[
                pl.BlockSpec((tile, width), lambda i, place: (jnp.minimum(i, steps - 1), 0)),
                pl.BlockSpec((tile, width), lambda i, place: (jnp.maximum(i - steps, 0), 0)),
                pl.BlockSpec((1, width), lambda i, place: (0, 0)),
            ],
            scratch_shapes=[pltpu.VMEM((2 * shard, width), BF16), pltpu.SemaphoreType.DMA((2,))],
        ),
        out_shape=[
            jax.ShapeDtypeStruct((shard, width), BF16),
            jax.ShapeDtypeStruct((shard, width), F32),
            jax.ShapeDtypeStruct((1, width), F32),
        ],
        compiler_params=pltpu.CompilerParams(vmem_limit_bytes=21 * 2**20),
        cost_estimate=pl.CostEstimate(
            flops=8 * shard * shard * width, bytes_accessed=8 * shard * shard + 14 * shard * width, transcendentals=0
        ),
        name="second_pair",
    )(place, matrix, before, *ends, *mids, after)


def hold_kernel(*refs):
    refs[-1][...] = jnp.zeros_like(refs[-1])


def hold(width, *others):
    return pl.pallas_call(
        hold_kernel,
        in_specs=[pl.BlockSpec(memory_space=pl.ANY)] * len(others),
        out_specs=pl.BlockSpec(memory_space=pltpu.VMEM),
        out_shape=jax.ShapeDtypeStruct((1, width), F32),
        compiler_params=pltpu.CompilerParams(vmem_limit_bytes=2**20),
        name="hold",
    )(*others)


def pipelined(inverse_rows, hess_weight, pruned_start, dual_start, prune_mask, dual_rate):
    shard, out = hess_weight.shape
    width = out // CHUNKS
    tile = 1344
    col = lax.axis_index("col")
    row = lax.axis_index("row")
    own_pair = col // 2
    at_end = (col == 0) | (col == 3)
    core = row % 2
    other_x = 1 - row // 2
    as_i32 = lambda *values: jnp.stack([jnp.asarray(value, jnp.int32) for value in values])
    first_place = as_i32(own_pair, col % 2)
    far_place = as_i32(1 - own_pair, at_end, 2 * other_x + 1 - core, 2 * other_x + core)
    near_place = as_i32(1 - own_pair, at_end, row + 1 - 2 * core, row)

    step_size = (0.5 + 0.25 * dual_rate.astype(F32))[None, :]
    parts = [slice(chunk * width, (chunk + 1) * width) for chunk in range(CHUNKS)]
    projected = [pruned_start[:, part] for part in parts]
    scaled = [dual_start[:, part] for part in parts]

    def right_side(chunk):
        return (hess_weight[:, parts[chunk]] + projected[chunk] - scaled[chunk]).astype(BF16)

    def gather(own):
        outer = lax.ppermute(own, "col", OUTER)
        inner = lax.ppermute(own, "col", INNER)
        next_inner = lax.ppermute(outer, "col", INNER)
        end_a = lax.ppermute(inner, "col", ENDS)
        return own, outer, end_a, (inner, next_inner)

    def finish(gathered, zeros):
        own, outer, end_a, (inner, next_inner) = gathered
        passed = (next_inner.astype(F32) + zeros).astype(BF16)
        end_b = lax.ppermute(passed, "col", ENDS)
        return own, outer, (end_a, end_b), (inner, next_inner)

    def multiply_rest(gathered, before, after, upcoming):
        _, _, ends, mids = gathered
        send_far, keep_far, _ = second_pair(far_place, inverse_rows, before, ends, mids, after, tile)
        far = keep_far + lax.ppermute(send_far, "row", CORE).astype(F32)
        if upcoming is not None:
            far = far + hold(width, upcoming[1], upcoming[3][0])
        far = far.astype(BF16)
        send_near, keep_near, zeros = second_pair(near_place, inverse_rows, before, ends, mids, far, tile)
        sums = keep_near, lax.ppermute(send_near, "row", CORE), lax.ppermute(far, "row", ACROSS)
        return sums, send_near, zeros

    def update(chunk, sums, zeros):
        near, core_sum, far_sum = sums
        step = step_size[:, parts[chunk]] + zeros
        iterate = near + core_sum.astype(F32) + far_sum.astype(F32)
        projected[chunk] = jnp.where(prune_mask[:, parts[chunk]] == 1, iterate + scaled[chunk], 0.0)
        scaled[chunk] = scaled[chunk] + step * (iterate - projected[chunk])

    gathered = gather(right_side(0))
    before, after = first_pair(first_place, inverse_rows, *gathered[:2], (gathered[3][0],), 1344)
    gathered = finish(gathered, 0.0)
    waiting = (right_side(1).astype(F32) + after).astype(BF16)
    for step in range(ITERS * CHUNKS):
        chunk, last = step % CHUNKS, step == ITERS * CHUNKS - 1
        upcoming = None if last else gather(waiting)
        sums, sent, zeros = multiply_rest(gathered, before, after, upcoming)
        if last:
            zeros = hold(width, sums[2])
        else:
            unread = (sent, sums[2], upcoming[2], upcoming[3][1])
            before, after_first = first_pair(first_place, inverse_rows, *upcoming[:2], unread, 1344)
            gathered = finish(upcoming, zeros)
            zeros = after_first
        update(chunk, sums, zeros)
        waiting = after = right_side(chunk)
    whole = [jnp.pad(half[0], ((0, 0), (0, width))) for half in (projected, scaled)]
    return tuple(
        lax.dynamic_update_slice(full, half[1], (0, width)) for full, half in zip(whole, (projected, scaled))
    )


def plain(inverse_rows, hess_weight, pruned_start, dual_start, prune_mask, dual_rate):
    kept = prune_mask.astype(F32)
    step_size = 0.5 + 0.25 * dual_rate.astype(F32)
    projected = pruned_start
    scaled = dual_start
    for iteration in range(ITERS):
        right_side = (hess_weight + projected - scaled).astype(BF16)
        partial_value = jnp.dot(
            inverse_rows,
            lax.all_gather(right_side, "col", axis=0, tiled=True),
            preferred_element_type=F32,
        )
        iterate = lax.psum_scatter(partial_value, "row", scatter_dimension=0, tiled=True)
        projected = kept * (iterate + scaled)
        scaled = scaled + step_size[None, :] * (iterate - projected)
    return (projected, scaled)


def solution(mesh):
    in_specs = (
        P(("layer", "col"), "row"),
        P(("layer", "row", "col"), None),
        P(("layer", "row", "col"), None),
        P(("layer", "row", "col"), None),
        P(("layer", "row", "col"), None),
        P("layer"),
    )
    out_specs = (P(("layer", "row", "col"), None), P(("layer", "row", "col"), None))
    four_by_four = mesh.shape["row"] == 4 and mesh.shape["col"] == 4
    local = pipelined if four_by_four else plain
    return jax.shard_map(local, mesh=mesh, in_specs=in_specs, out_specs=out_specs, check_vma=False)
```

```python
import jax
import jax.numpy as jnp
from jax import lax
from jax.experimental import pallas as pl
from jax.experimental.pallas import tpu as pltpu
from jax.sharding import PartitionSpec as P

ITERS = 3
CHUNKS = 2
BF16 = jnp.bfloat16
F32 = jnp.float32

OUTER = [(0, 1), (1, 0), (2, 3), (3, 2)]
INNER = [(1, 2), (2, 1)]
ENDS = [(1, 0), (2, 3)]
CORE = [(0, 1), (1, 0), (2, 3), (3, 2)]
ACROSS = [(0, 2), (2, 0), (1, 3), (3, 1)]


def first_pair_kernel(place, matrix, own, near, *rest):
    out, token, pair, sems = rest[-4:]

    shard = own.shape[0]

    @pl.when(pl.program_id(0) == 0)
    def _():
        here = pl.multiple_of(place[1] * shard, 16)
        there = pl.multiple_of((1 - place[1]) * shard, 16)
        copies = [
            pltpu.make_async_copy(own, pair.at[pl.ds(here, shard)], sems.at[0]),
            pltpu.make_async_copy(near, pair.at[pl.ds(there, shard)], sems.at[1]),
        ]
        for copy in copies:
            copy.start()
        for copy in copies:
            copy.wait()

    out[...] = jnp.dot(matrix[...], pair[...], preferred_element_type=F32)
    token[...] = jnp.zeros_like(token)


def first_pair(place, matrix, own, near, after, tile):
    shard, width = own.shape
    slab = matrix.shape[0]
    return pl.pallas_call(
        first_pair_kernel,
        grid_spec=pltpu.PrefetchScalarGridSpec(
            num_scalar_prefetch=1,
            grid=(slab // tile,),
            in_specs=[
                pl.BlockSpec((tile, 2 * shard), lambda i, place: (i, place[0])),
            ]
            + [pl.BlockSpec(memory_space=pl.ANY)] * (2 + len(after)),
            out_specs=[
                pl.BlockSpec((tile, width), lambda i, place: (i, 0)),
                pl.BlockSpec((1, width), lambda i, place: (0, 0)),
            ],
            scratch_shapes=[pltpu.VMEM((2 * shard, width), BF16), pltpu.SemaphoreType.DMA((2,))],
        ),
        out_shape=[jax.ShapeDtypeStruct((slab, width), F32), jax.ShapeDtypeStruct((1, width), F32)],
        compiler_params=pltpu.CompilerParams(vmem_limit_bytes=20 * 2**20),
        cost_estimate=pl.CostEstimate(
            flops=4 * slab * shard * width, bytes_accessed=4 * slab * shard + 4 * slab * width, transcendentals=0
        ),
        name="first_pair",
    )(place, matrix, own, near, *after)


def second_pair_kernel(place, matrix, before, end_a, end_b, mid_a, mid_b, after, send, keep, token, pair, sems):
    shard = end_a.shape[0]
    step = pl.program_id(0)
    half_steps = pl.num_programs(0) // 2

    @pl.when(step == 0)
    def _():
        here = pl.multiple_of((1 - place[0]) * shard, 16)
        there = pl.multiple_of(place[0] * shard, 16)

        def fetch(a, b):
            copies = [
                pltpu.make_async_copy(a, pair.at[pl.ds(here, shard)], sems.at[0]),
                pltpu.make_async_copy(b, pair.at[pl.ds(there, shard)], sems.at[1]),
            ]
            for copy in copies:
                copy.start()
            for copy in copies:
                copy.wait()

        @pl.when(place[1] == 1)
        def _():
            fetch(end_a, end_b)

        @pl.when(place[1] == 0)
        def _():
            fetch(mid_a, mid_b)

    token[...] = jnp.zeros_like(token)
    total = before[...] + jnp.dot(matrix[...], pair[...], preferred_element_type=F32)

    @pl.when(step < half_steps)
    def _():
        send[...] = total.astype(BF16)

    @pl.when(step >= half_steps)
    def _():
        keep[...] = total


def second_pair(place, matrix, before, ends, mids, after, tile):
    shard, width = ends[0].shape
    steps = shard // tile

    def row(i, place):
        return jnp.where(i < steps, place[2], place[3]) * steps + lax.rem(i, steps)

    return pl.pallas_call(
        second_pair_kernel,
        grid_spec=pltpu.PrefetchScalarGridSpec(
            num_scalar_prefetch=1,
            grid=(2 * steps,),
            in_specs=[
                pl.BlockSpec((tile, 2 * shard), lambda i, place: (row(i, place), place[0])),
                pl.BlockSpec((tile, width), lambda i, place: (row(i, place), 0)),
            ]
            + [pl.BlockSpec(memory_space=pl.ANY)] * 5,
            out_specs=[
                pl.BlockSpec((tile, width), lambda i, place: (jnp.minimum(i, steps - 1), 0)),
                pl.BlockSpec((tile, width), lambda i, place: (jnp.maximum(i - steps, 0), 0)),
                pl.BlockSpec((1, width), lambda i, place: (0, 0)),
            ],
            scratch_shapes=[pltpu.VMEM((2 * shard, width), BF16), pltpu.SemaphoreType.DMA((2,))],
        ),
        out_shape=[
            jax.ShapeDtypeStruct((shard, width), BF16),
            jax.ShapeDtypeStruct((shard, width), F32),
            jax.ShapeDtypeStruct((1, width), F32),
        ],
        compiler_params=pltpu.CompilerParams(vmem_limit_bytes=21 * 2**20),
        cost_estimate=pl.CostEstimate(
            flops=8 * shard * shard * width, bytes_accessed=8 * shard * shard + 14 * shard * width, transcendentals=0
        ),
        name="second_pair",
    )(place, matrix, before, *ends, *mids, after)


def hold_kernel(*refs):
    refs[-1][...] = jnp.zeros_like(refs[-1])


def hold(width, *others):
    return pl.pallas_call(
        hold_kernel,
        in_specs=[pl.BlockSpec(memory_space=pl.ANY)] * len(others),
        out_specs=pl.BlockSpec(memory_space=pltpu.VMEM),
        out_shape=jax.ShapeDtypeStruct((1, width), F32),
        compiler_params=pltpu.CompilerParams(vmem_limit_bytes=2**20),
        name="hold",
    )(*others)


def pipelined(inverse_rows, hess_weight, pruned_start, dual_start, prune_mask, dual_rate):
    shard, out = hess_weight.shape
    width = out // CHUNKS
    tile = 1344
    col = lax.axis_index("col")
    row = lax.axis_index("row")
    own_pair = col // 2
    at_end = (col == 0) | (col == 3)
    core = row % 2
    other_x = 1 - row // 2
    as_i32 = lambda *values: jnp.stack([jnp.asarray(value, jnp.int32) for value in values])
    first_place = as_i32(own_pair, col % 2)
    far_place = as_i32(1 - own_pair, at_end, 2 * other_x + 1 - core, 2 * other_x + core)
    near_place = as_i32(1 - own_pair, at_end, row + 1 - 2 * core, row)

    step_size = (0.5 + 0.25 * dual_rate.astype(F32))[None, :]
    parts = [slice(chunk * width, (chunk + 1) * width) for chunk in range(CHUNKS)]
    projected = [pruned_start[:, part] for part in parts]
    scaled = [dual_start[:, part] for part in parts]

    def right_side(chunk):
        return (hess_weight[:, parts[chunk]] + projected[chunk] - scaled[chunk]).astype(BF16)

    def gather(own):
        outer = lax.ppermute(own, "col", OUTER)
        inner = lax.ppermute(own, "col", INNER)
        next_inner = lax.ppermute(outer, "col", INNER)
        end_a = lax.ppermute(inner, "col", ENDS)
        return own, outer, end_a, (inner, next_inner)

    def finish(gathered, zeros):
        own, outer, end_a, (inner, next_inner) = gathered
        passed = (next_inner.astype(F32) + zeros).astype(BF16)
        end_b = lax.ppermute(passed, "col", ENDS)
        return own, outer, (end_a, end_b), (inner, next_inner)

    def multiply_rest(gathered, before, after, upcoming):
        _, _, ends, mids = gathered
        send_far, keep_far, _ = second_pair(far_place, inverse_rows, before, ends, mids, after, tile)
        far = keep_far + lax.ppermute(send_far, "row", CORE).astype(F32)
        if upcoming is not None:
            far = far + hold(width, upcoming[1], upcoming[3][0])
        far = far.astype(BF16)
        send_near, keep_near, zeros = second_pair(near_place, inverse_rows, before, ends, mids, far, tile)
        sums = keep_near, lax.ppermute(send_near, "row", CORE), lax.ppermute(far, "row", ACROSS)
        return sums, send_near, zeros

    def update(chunk, sums, zeros):
        near, core_sum, far_sum = sums
        step = step_size[:, parts[chunk]] + zeros
        iterate = near + core_sum.astype(F32) + far_sum.astype(F32)
        projected[chunk] = jnp.where(prune_mask[:, parts[chunk]] == 1, iterate + scaled[chunk], 0.0)
        scaled[chunk] = scaled[chunk] + step * (iterate - projected[chunk])

    gathered = gather(right_side(0))
    before, after = first_pair(first_place, inverse_rows, *gathered[:2], (gathered[3][0],), 1344)
    gathered = finish(gathered, 0.0)
    waiting = (right_side(1).astype(F32) + after).astype(BF16)
    for step in range(ITERS * CHUNKS):
        chunk, last = step % CHUNKS, step == ITERS * CHUNKS - 1
        upcoming = None if last else gather(waiting)
        sums, sent, zeros = multiply_rest(gathered, before, after, upcoming)
        if last:
            zeros = hold(width, sums[2])
        else:
            unread = (sent, upcoming[2], upcoming[3][1])
            before, after_first = first_pair(first_place, inverse_rows, *upcoming[:2], unread, 1344)
            gathered = finish(upcoming, zeros)
            zeros = after_first
        update(chunk, sums, zeros)
        waiting = after = right_side(chunk)
    whole = [jnp.pad(half[0], ((0, 0), (0, width))) for half in (projected, scaled)]
    return tuple(
        lax.dynamic_update_slice(full, half[1], (0, width)) for full, half in zip(whole, (projected, scaled))
    )


def plain(inverse_rows, hess_weight, pruned_start, dual_start, prune_mask, dual_rate):
    kept = prune_mask.astype(F32)
    step_size = 0.5 + 0.25 * dual_rate.astype(F32)
    projected = pruned_start
    scaled = dual_start
    for iteration in range(ITERS):
        right_side = (hess_weight + projected - scaled).astype(BF16)
        partial_value = jnp.dot(
            inverse_rows,
            lax.all_gather(right_side, "col", axis=0, tiled=True),
            preferred_element_type=F32,
        )
        iterate = lax.psum_scatter(partial_value, "row", scatter_dimension=0, tiled=True)
        projected = kept * (iterate + scaled)
        scaled = scaled + step_size[None, :] * (iterate - projected)
    return (projected, scaled)


def solution(mesh):
    in_specs = (
        P(("layer", "col"), "row"),
        P(("layer", "row", "col"), None),
        P(("layer", "row", "col"), None),
        P(("layer", "row", "col"), None),
        P(("layer", "row", "col"), None),
        P("layer"),
    )
    out_specs = (P(("layer", "row", "col"), None), P(("layer", "row", "col"), None))
    four_by_four = mesh.shape["row"] == 4 and mesh.shape["col"] == 4
    local = pipelined if four_by_four else plain
    return jax.shard_map(local, mesh=mesh, in_specs=in_specs, out_specs=out_specs, check_vma=False)
```
